32 devices in a mesh: row: 8 (over y, x, core), col: 4 (over z).
Axes of the slice: x: 2, y: 2, z: 4, core: 2. Of those that a mesh axis runs over, the one named last changes fastest.
Arguments:
- gain_pair: float32 [2], replicated, may hold values from 0.5 to 2
- weight_up: bfloat16 [24576, 6144], P('row', 'col'), as said below
- weight_down: bfloat16 [6144, 24576], P('row', 'col'), as said below
- inputs_up: bfloat16 [1536, 6144], P('row', 'col'), may hold values from -8 to 8, as said below
- grads_up: bfloat16 [1536, 24576], P('col', 'row'), may hold values from -0.125 to 0.125, as said below
- inputs_down: bfloat16 [1536, 24576], P('row', 'col'), may hold values from -8 to 8, as said below
- grads_down: bfloat16 [1536, 6144], P('col', 'row'), may hold values from -0.125 to 0.125, as said below
- vector_up: float32 [6144], P('col'), may hold values from -6 to 6
- vector_down: float32 [24576], P('col'), may hold values from -6 to 6
Outputs:
- wgrad_up: bfloat16 [24576, 6144], P('row', 'col')
- wgrad_down: bfloat16 [6144, 24576], P('row', 'col')
- gain_grads: float32 [2], replicated
- left_up: float32 [24576], P('row')
- right_up: float32 [6144], P('col')
- left_down: float32 [6144], P('row')
- right_down: float32 [24576], P('col')
The draws below stay inside these ranges and needn't reach their ends.
Inputs may be any that keep to these rules, and one draw needn't show every extreme that they name: `weight_up`: drawn afresh from the seed for every entry. `weight_down`: drawn afresh from the seed for every entry. `inputs_up`: drawn afresh from the seed for every entry. `inputs_down`: drawn afresh from the seed for every entry. `grads_up`: drawn afresh from the seed for every entry. `grads_down`: drawn afresh from the seed for every entry.
All inputs are finite; a program needn't handle non-finite values.
Results may differ from the reference program's by a relative error of at most 0.007.
Values may be sent and summed in bfloat16 or wider, within the bound.
No kernel may reach another device: no remote copies, remote signals or barrier semaphores. Data moves between devices by JAX's collectives and lax.ppermute only.
A program may use at most 192 MiB of HBM per device.

```python
import jax
import jax.numpy as jnp
from jax import lax

D = 6144
FF = 24576
ITERS = 2
TOKENS = 1536


def shared(key, tag, count, factor):
    base = jax.random.normal(jax.random.fold_in(key, tag), (count,), jnp.float32)
    return jnp.clip(base, -4.0, 4.0) * factor


def noise(key, tag, shape, limit):
    return jnp.clip(jax.random.normal(jax.random.fold_in(key, tag), shape, jnp.float32), -limit, limit)


def draw_weight_up(key, part):
    rows_q = shared(key, 11, FF, 0.1)
    cols_p = shared(key, 12, D, 0.1)
    return (noise(key, 103, (FF, D), 6.0) * D ** (-0.5) + 0.05 * rows_q[:, None] * cols_p[None, :]).astype(jnp.bfloat16)


def draw_inputs_up(key, part):
    tokens_a = shared(key, 13, TOKENS, 1.0)
    cols_p = shared(key, 12, D, 0.1)
    return jnp.clip(noise(key, 101, (TOKENS, D), 6.0) + tokens_a[:, None] * cols_p[None, :], -8.0, 8.0).astype(jnp.bfloat16)


def draw_grads_up(key, part):
    tokens_a = shared(key, 13, TOKENS, 1.0)
    rows_q = shared(key, 11, FF, 0.1)
    return (jnp.clip(noise(key, 102, (TOKENS, FF), 6.0) + tokens_a[:, None] * rows_q[None, :], -8.0, 8.0) / 64.0).astype(jnp.bfloat16)


def draw_weight_down(key, part):
    rows_q = shared(key, 21, D, 0.1)
    cols_p = shared(key, 22, FF, 0.1)
    return (noise(key, 203, (D, FF), 6.0) * FF ** (-0.5) + 0.05 * rows_q[:, None] * cols_p[None, :]).astype(jnp.bfloat16)


def draw_inputs_down(key, part):
    tokens_a = shared(key, 23, TOKENS, 1.0)
    cols_p = shared(key, 22, FF, 0.1)
    return jnp.clip(noise(key, 201, (TOKENS, FF), 6.0) + tokens_a[:, None] * cols_p[None, :], -8.0, 8.0).astype(jnp.bfloat16)


def draw_grads_down(key, part):
    tokens_a = shared(key, 23, TOKENS, 1.0)
    rows_q = shared(key, 21, D, 0.1)
    return (jnp.clip(noise(key, 202, (TOKENS, D), 6.0) + tokens_a[:, None] * rows_q[None, :], -8.0, 8.0) / 64.0).astype(jnp.bfloat16)


def block_scale(key, extent, split, smallest, top_value):
    level = 1.0
    for position, parts in split:
        draws = jax.random.uniform(jax.random.fold_in(jax.random.fold_in(key, 6), position), (parts,), jnp.float32, smallest / len(split), top_value / len(split))
        level = level * jnp.repeat(jnp.exp(draws), extent[position] // parts).reshape((-1,) + (1,) * (len(extent) - 1 - position))
    return level


def normal_values(own_key, dims, scale, most, shards=(), held_as=jnp.bfloat16):
    factor_of = block_scale(own_key, dims, shards, -0.22, 0.18) if shards else 1.0
    array = jax.random.normal(own_key, dims, jnp.float32) * scale * factor_of
    return jnp.minimum(jnp.maximum(array, -most), most).astype(held_as)


def setup_inputs(seed: int = 0) -> dict:
    key_list = jax.random.split(jax.random.key(seed), 10)
    gain_pair = jnp.clip(jax.random.uniform(key_list[0], (2,), jnp.float32, 0.5, 2.0), 0.5, 2.0)
    weight_up = draw_weight_up(jax.random.fold_in(key_list[9], 71), 0)
    weight_down = draw_weight_down(jax.random.fold_in(key_list[9], 71), 0)
    inputs_up = draw_inputs_up(jax.random.fold_in(key_list[9], 71), 0)
    grads_up = draw_grads_up(jax.random.fold_in(key_list[9], 71), 0)
    inputs_down = draw_inputs_down(jax.random.fold_in(key_list[9], 71), 0)
    grads_down = draw_grads_down(jax.random.fold_in(key_list[9], 71), 0)
    vector_up = normal_values(key_list[7], (D,), 1.0, 6.0, ((0, 4),), jnp.float32)
    vector_down = normal_values(key_list[8], (FF,), 1.0, 6.0, ((0, 4),), jnp.float32)
    return {"gain_pair": gain_pair, "weight_up": weight_up, "weight_down": weight_down, "inputs_up": inputs_up, "grads_up": grads_up, "inputs_down": inputs_down, "grads_down": grads_down, "vector_up": vector_up, "vector_down": vector_down}


def project(weight, inputs, grads, vector, gain):
    grad_w = lax.dot_general(grads, inputs, (((0,), (0,)), ((), ())), preferred_element_type=jnp.float32)
    right = vector
    left = vector
    left_b = vector.astype(jnp.bfloat16)
    sigma = jnp.float32(1.0)
    for step in range(ITERS):
        right_b = right.astype(jnp.bfloat16)
        prod_s = jnp.dot(weight, right_b, preferred_element_type=jnp.float32)
        left = prod_s / jnp.sqrt(jnp.sum(prod_s * prod_s) + 1e-06)
        left_b = left.astype(jnp.bfloat16)
        prod_t = jnp.dot(left_b, weight, preferred_element_type=jnp.float32)
        if step + 1 < ITERS:
            right = prod_t
        else:
            sigma = jnp.sqrt(jnp.sum(prod_t * prod_t) + 1e-06)
            right = prod_t / sigma
    inner = jnp.sum(grad_w * weight.astype(jnp.float32))
    outer = left_b.astype(jnp.float32)[:, None] * right[None, :]
    wgrad = (gain / sigma * grad_w - gain * inner / (sigma * sigma) * outer).astype(jnp.bfloat16)
    return (wgrad, inner / sigma, left, right)

def reference(gain_pair, weight_up, weight_down, inputs_up, grads_up, inputs_down, grads_down, vector_up, vector_down):
    wgrad_up, gain_a, left_up, right_up = project(weight_up, inputs_up, grads_up, vector_up, gain_pair[0])
    wgrad_down, gain_b, left_down, right_down = project(weight_down, inputs_down, grads_down, vector_down, gain_pair[1])
    gain_grads = jnp.stack([gain_a, gain_b]).astype(jnp.float32)
    return (wgrad_up, wgrad_down, gain_grads, left_up, right_up, left_down, right_down)
```

```python
import functools

import jax
import jax.numpy as jnp
from jax import lax
from jax.experimental import pallas as pl
from jax.experimental.pallas import tpu as pltpu
from jax.sharding import PartitionSpec as P

EPS = 1e-06
LANES = 128
PARAMS = pltpu.CompilerParams(vmem_limit_bytes=56 * 1024 * 1024)
F32 = jnp.float32
BF16 = jnp.bfloat16


def all_sum(value, axis, size):
    step = 1
    while step < size:
        value = value + lax.ppermute(value, axis, [(i, i ^ step) for i in range(size)])
        step *= 2
    return value


def exchange(value, axis, size):
    return [value] + [
        lax.ppermute(value, axis, [(i, i ^ k) for i in range(size)]) for k in range(1, size)
    ]


def tree(terms):
    while len(terms) > 1:
        terms = [terms[i] + terms[i + 1] for i in range(0, len(terms), 2)]
    return terms[0]


def fence(*values):
    return lax.optimization_barrier(values)


def tile_of(extent, most):
    tile = min(extent, most)
    while extent % tile:
        tile -= LANES
    return tile


def column_of(row):
    return jnp.broadcast_to(row, (LANES, row.shape[1])).T


def row_of(block):
    return jnp.sum(block.T, axis=0, keepdims=True)


def norm_of(squares):
    return jnp.sqrt(jnp.sum(squares, axis=1, keepdims=True) + EPS)


def whole(array):
    return pl.BlockSpec(array.shape, lambda *_: (0,) * array.ndim)


def row_blocks(weights):
    steps = weights[1].shape[0] // LANES
    return [w.shape[0] // steps for w in weights], steps


def left_product(rights, weights):
    heights, steps = row_blocks(weights)
    extents = [w.shape[0] for w in weights]

    def kernel(v_up_ref, v_down_ref, w_up_ref, w_down_ref, out_ref):
        step = pl.program_id(0)
        offset = 0
        for k, (w_ref, v_ref) in enumerate(((w_up_ref, v_up_ref), (w_down_ref, v_down_ref))):
            height, depth = w_ref.shape
            sums = []
            for top in range(0, height, 64):
                total = jnp.zeros((64, LANES), F32)
                for c in range(0, depth, LANES):
                    v = v_ref[:, c : c + LANES].astype(BF16).astype(F32)
                    total += w_ref[top : top + 64, c : c + LANES].astype(F32) * v
                sums.append(total)
            start = pl.multiple_of(offset + step * height, LANES)
            out_ref[:, pl.ds(start, height)] = row_of(jnp.concatenate(sums))
            offset += extents[k]

    return pl.pallas_call(
        kernel,
        grid=(steps,),
        in_specs=[whole(r) for r in rights]
        + [pl.BlockSpec((heights[k], weights[k].shape[1]), lambda i: (i, 0)) for k in range(2)],
        out_specs=pl.BlockSpec((1, sum(extents)), lambda i: (0, 0)),
        out_shape=jax.ShapeDtypeStruct((1, sum(extents)), F32),
        compiler_params=PARAMS,
    )(*rights, *weights)


def right_product(terms, weights):
    heights, steps = row_blocks(weights)
    extents = [w.shape[0] for w in weights]
    spans = [w.shape[1] for w in weights]
    count = len(terms)

    def kernel(*refs):
        w_refs, (left_ref, out_ref) = refs[count : count + 2], refs[count + 2 :]
        step = pl.program_id(0)

        @pl.when(step == 0)
        def _():
            out_ref[...] = jnp.zeros_like(out_ref)
            left_ref[...] = tree([ref[...] for ref in refs[:count]])

        row = lane = 0
        for k in range(2):
            start = pl.multiple_of(row + step * heights[k], LANES)
            left = left_ref[:, pl.ds(start, heights[k])]
            column = column_of(left.astype(BF16).astype(F32))
            for c in range(0, spans[k], LANES):
                total = jnp.zeros((8, LANES), F32)
                for top in range(0, heights[k], 64):
                    product = w_refs[k][top : top + 64, c : c + LANES].astype(F32) * column[top : top + 64]
                    total += jnp.sum(product.reshape(8, 8, LANES), axis=0)
                out_ref[:, lane + c : lane + c + LANES] += jnp.sum(total, axis=0, keepdims=True)
            squares = left * left
            here = slice(sum(spans) + k * LANES, sum(spans) + (k + 1) * LANES)
            for c in range(0, heights[k], LANES):
                out_ref[:, here] += squares[:, c : c + LANES]
            row += extents[k]
            lane += spans[k]

    total = sum(spans) + 2 * LANES
    return pl.pallas_call(
        kernel,
        grid=(steps,),
        in_specs=[whole(t) for t in terms]
        + [pl.BlockSpec((heights[k], spans[k]), lambda i: (i, 0)) for k in range(2)],
        out_specs=[pl.BlockSpec((1, sum(extents)), lambda i: (0, 0)), pl.BlockSpec((1, total), lambda i: (0, 0))],
        out_shape=[jax.ShapeDtypeStruct((1, sum(extents)), F32), jax.ShapeDtypeStruct((1, total), F32)],
        compiler_params=PARAMS,
    )(*terms, *weights)


def scale_right(total, spans):
    def kernel(total_ref, up_ref, down_ref, squares_ref):
        lane = 0
        for k, ref in enumerate((up_ref, down_ref)):
            here = sum(spans) + k * LANES
            ref[...] = total_ref[:, lane : lane + spans[k]] / norm_of(total_ref[:, here : here + LANES])
            squares = jnp.zeros((1, LANES), F32)
            for c in range(0, spans[k], LANES):
                squares += ref[:, c : c + LANES] * ref[:, c : c + LANES]
            squares_ref[k : k + 1, :] = squares
            lane += spans[k]

    return pl.pallas_call(
        kernel,
        out_shape=[jax.ShapeDtypeStruct((1, span), F32) for span in spans]
        + [jax.ShapeDtypeStruct((2, LANES), F32)],
        compiler_params=PARAMS,
    )(total)


def grad_chunk(order, blocks, inputs, weight, chunk, buffer, inner, which):
    count = len(blocks)
    tokens, width = blocks[0].shape
    depth, columns = inputs.shape
    tile = tile_of(columns, 512)

    def kernel(order_ref, *refs):
        x_ref, w_ref, before_ref = refs[count : count + 3]
        g_ref, inner_ref, turned = refs[-3:]

        @pl.when(pl.program_id(0) == 0)
        def _():
            inner_ref[...] = before_ref[...]
            for slot in range(count):
                start = pl.multiple_of(order_ref[slot] * tokens, LANES)
                turned[:, pl.ds(start, tokens)] = refs[slot][...].T

        here = slice(8 * which, 8 * which + 8)
        total = jnp.dot(turned[...], x_ref[...], preferred_element_type=F32)
        g_ref[...] = total.astype(g_ref.dtype)
        product = total * w_ref[...].astype(F32)
        product = jnp.sum(product.reshape(-1, 8, tile), axis=0)
        inner_ref[here, :] += sum(product[:, c : c + LANES] for c in range(0, tile, LANES))

    in_specs = [pl.BlockSpec((tokens, width), lambda j, o: (0, 0)) for _ in blocks]
    in_specs += [
        pl.BlockSpec((depth, tile), lambda j, o: (0, j)),
        pl.BlockSpec((width, tile), lambda j, o: (chunk, j)),
        pl.BlockSpec((16, LANES), lambda j, o: (0, 0)),
    ]
    operands = [order, *blocks, inputs, weight, inner]
    aliases = {}
    if buffer is not None:
        in_specs.append(pl.BlockSpec(memory_space=pl.ANY))
        operands.append(buffer)
        aliases = {count + 4: 0}
    return pl.pallas_call(
        kernel,
        grid_spec=pltpu.PrefetchScalarGridSpec(
            num_scalar_prefetch=1,
            grid=(columns // tile,),
            in_specs=in_specs,
            out_specs=[
                pl.BlockSpec((width, tile), lambda j, o: (chunk, j)),
                pl.BlockSpec((16, LANES), lambda j, o: (0, 0)),
            ],
            scratch_shapes=[pltpu.VMEM((width, depth), BF16)],
        ),
        out_shape=[
            jax.ShapeDtypeStruct(weight.shape, BF16),
            jax.ShapeDtypeStruct((16, LANES), F32),
        ],
        input_output_aliases=aliases,
        compiler_params=PARAMS,
    )(*operands)


def finish(grads, left, norms, rights, squares, inners, gains):
    heights, steps = row_blocks(grads)
    extents = [g.shape[0] for g in grads]
    spans = [g.shape[1] for g in grads]
    count = len(squares)

    def kernel(left_ref, norms_ref, *refs):
        v_refs, refs = refs[:2], refs[2:]
        square_refs, refs = refs[:count], refs[count:]
        inner_refs, refs = refs[:count], refs[count:]
        gains_ref, refs = refs[0], refs[1:]
        g_refs, out_refs, gain_ref = refs[:2], refs[2:4], refs[4]
        step = pl.program_id(0)
        square = tree([ref[...] for ref in square_refs])
        inner = tree([ref[...] for ref in inner_refs])
        row = 0
        for k in range(2):
            sigma = norm_of(square[k : k + 1])
            gw = jnp.sum(jnp.sum(inner[8 * k : 8 * k + 8], axis=0, keepdims=True), axis=1, keepdims=True)
            gain = gains_ref[k : k + 1, :1]
            scale = gain / sigma
            slope = gain * gw / (sigma * sigma)
            gain_ref[k : k + 1, :] = jnp.broadcast_to(gw / sigma, (1, LANES))
            start = pl.multiple_of(row + step * heights[k], LANES)
            norm = norm_of(norms_ref[:, k * LANES : (k + 1) * LANES])
            column = column_of((left_ref[:, pl.ds(start, heights[k])] / norm).astype(BF16).astype(F32))
            for c in range(0, spans[k], LANES):
                here = slice(c, c + LANES)
                v = slope * (v_refs[k][:, here] / sigma)
                out_refs[k][:, here] = (scale * g_refs[k][:, here].astype(F32) - column * v).astype(BF16)
            row += extents[k]

    operands = [left, norms, *rights, *squares, *inners, gains]
    blocks = [pl.BlockSpec((heights[k], spans[k]), lambda i: (i, 0)) for k in range(2)]
    return pl.pallas_call(
        kernel,
        grid=(steps,),
        in_specs=[whole(o) for o in operands] + blocks,
        out_specs=blocks + [pl.BlockSpec((2, LANES), lambda i: (0, 0))],
        out_shape=[jax.ShapeDtypeStruct(g.shape, BF16) for g in grads] + [jax.ShapeDtypeStruct((2, LANES), F32)],
        compiler_params=PARAMS,
    )(*operands, *grads)


def local(
    rows,
    cols,
    gain_pair,
    weight_up,
    weight_down,
    inputs_up,
    grads_up,
    inputs_down,
    grads_down,
    vector_up,
    vector_down,
):
    weights = (weight_up, weight_down)
    inputs_all = (
        lax.all_gather(inputs_up, "row", axis=0, tiled=True),
        lax.all_gather(inputs_down, "row", axis=0, tiled=True),
    )
    extents = (weight_up.shape[0], weight_down.shape[0])
    spans = (weight_up.shape[1], weight_down.shape[1])
    ring = [(i, (i + 1) % cols) for i in range(cols)]
    order = lax.rem(lax.axis_index("col") - jnp.arange(cols, dtype=jnp.int32) + cols, jnp.int32(cols))
    gains = jnp.broadcast_to(gain_pair[:, None], (2, LANES))

    unit = grads_up.shape[1] // 6
    chunks = [
        [grads_down, grads_up[:, : 2 * unit]],
        [grads_up[:, 2 * unit : 4 * unit]],
        [grads_up[:, 4 * unit : 5 * unit]],
        [grads_up[:, 5 * unit :]],
    ]
    streams = [[chunk] for chunk in chunks]

    def hop(pieces):
        return [lax.ppermute(piece, "col", ring) for piece in pieces]

    def advance(number, *others):
        held, *others = fence(streams[number][-1], *others)
        streams[number][-1] = held
        streams[number].append(hop(held))
        return others

    def land(number, *others):
        held, *others = fence(streams[number][-1], *others)
        streams[number][-1] = held
        return others

    grad_ws = [None, None]
    inner = jnp.zeros((16, LANES), F32)

    def multiply(k, number, place, chunk):
        slots = [pieces[place] for pieces in streams[number]]
        return grad_chunk(order, slots, inputs_all[k], weights[k], chunk, grad_ws[k], inner, k)

    streams[0].append(hop(chunks[0]))
    streams[1].append(hop(chunks[1]))
    part = left_product((vector_up[None, :], vector_down[None, :]), weights)
    terms = exchange(part, "col", cols)
    (terms,) = advance(0, terms)
    (terms,) = advance(1, terms)
    left, total = right_product(terms, weights)
    *rights, _ = scale_right(all_sum(total, "row", rows), spans)
    part = left_product(rights, weights)
    (part,) = advance(0, part)
    terms = exchange(part, "col", cols)
    (terms,) = advance(1, terms)
    left, total = right_product(terms, weights)
    total = all_sum(total, "row", rows)
    for _ in range(cols - 4):
        (total,) = advance(0, total)
        (total,) = advance(1, total)
    (total,) = land(0, total)
    (total,) = advance(2, total)
    *rights, square = scale_right(total, spans)
    squares = exchange(square, "col", cols)
    (inner,) = advance(3, inner)
    grad_ws[0], inner = multiply(0, 0, 1, 0)
    (inner,) = land(1, inner)
    for step in range(cols - 2):
        (inner,) = advance(2, inner)
        if step == 0:
            grad_ws[0], inner = multiply(0, 1, 0, 1)
        (inner,) = advance(3, inner)
    grad_ws[1], inner = multiply(1, 0, 0, 0)
    (inner,) = land(2, inner)
    grad_ws[0], inner = multiply(0, 2, 0, 4)
    (inner,) = land(3, inner)
    grad_ws[0], inner = multiply(0, 3, 0, 5)
    inners = exchange(all_sum(inner, "row", rows), "col", cols)
    norms = total[:, sum(spans) :]
    wgrad_up, wgrad_down, gain_grads = finish(grad_ws, left, norms, rights, squares, inners, gains)

    norm = jnp.sqrt(jnp.sum(norms.reshape(2, LANES), axis=1) + EPS)
    sigma = jnp.sqrt(jnp.sum(tree(squares), axis=1) + EPS)
    left_up = left[0, : extents[0]] / norm[0]
    left_down = left[0, extents[0] :] / norm[1]
    right_up, right_down = (rights[k][0] / sigma[k] for k in range(2))
    return wgrad_up, wgrad_down, gain_grads[:, 0], left_up, right_up, left_down, right_down


def solution(mesh):
    in_specs = (
        P(),
        P("row", "col"),
        P("row", "col"),
        P("row", "col"),
        P("col", "row"),
        P("row", "col"),
        P("col", "row"),
        P("col"),
        P("col"),
    )
    out_specs = (P("row", "col"), P("row", "col"), P(), P("row"), P("col"), P("row"), P("col"))
    body = functools.partial(local, mesh.shape["row"], mesh.shape["col"])
    return jax.shard_map(body, mesh=mesh, in_specs=in_specs, out_specs=out_specs, check_vma=False)
```

```python
import functools

import jax
import jax.numpy as jnp
from jax import lax
from jax.experimental import pallas as pl
from jax.experimental.pallas import tpu as pltpu
from jax.sharding import PartitionSpec as P

EPS = 1e-06
LANES = 128
PARAMS = pltpu.CompilerParams(vmem_limit_bytes=28 * 1024 * 1024)
F32 = jnp.float32
BF16 = jnp.bfloat16


def all_sum(value, axis, size):
    step = 1
    while step < size:
        value = value + lax.ppermute(value, axis, [(i, i ^ step) for i in range(size)])
        step *= 2
    return value


def exchange(value, axis, size):
    return [value] + [
        lax.ppermute(value, axis, [(i, i ^ k) for i in range(size)]) for k in range(1, size)
    ]


def tree(terms):
    while len(terms) > 1:
        terms = [terms[i] + terms[i + 1] for i in range(0, len(terms), 2)]
    return terms[0]


def fence(*values):
    return lax.optimization_barrier(values)


def tile_of(extent, most):
    tile = min(extent, most)
    while extent % tile:
        tile -= LANES
    return tile


def column_of(row):
    return jnp.broadcast_to(row, (LANES, row.shape[1])).T


def row_of(block):
    return jnp.sum(block.T, axis=0, keepdims=True)


def norm_of(squares):
    return jnp.sqrt(jnp.sum(squares, axis=1, keepdims=True) + EPS)


def whole(array):
    return pl.BlockSpec(array.shape, lambda *_: (0,) * array.ndim)


def row_blocks(weights):
    steps = weights[1].shape[0] // LANES
    return [w.shape[0] // steps for w in weights], steps


def left_product(rights, weights):
    heights, steps = row_blocks(weights)
    extents = [w.shape[0] for w in weights]

    def kernel(v_up_ref, v_down_ref, w_up_ref, w_down_ref, out_ref):
        step = pl.program_id(0)
        offset = 0
        for k, (w_ref, v_ref) in enumerate(((w_up_ref, v_up_ref), (w_down_ref, v_down_ref))):
            height, depth = w_ref.shape
            sums = []
            for top in range(0, height, 64):
                total = jnp.zeros((64, LANES), F32)
                for c in range(0, depth, LANES):
                    v = v_ref[:, c : c + LANES].astype(BF16).astype(F32)
                    total += w_ref[top : top + 64, c : c + LANES].astype(F32) * v
                sums.append(total)
            start = pl.multiple_of(offset + step * height, LANES)
            out_ref[:, pl.ds(start, height)] = row_of(jnp.concatenate(sums))
            offset += extents[k]

    return pl.pallas_call(
        kernel,
        grid=(steps,),
        in_specs=[whole(r) for r in rights]
        + [pl.BlockSpec((heights[k], weights[k].shape[1]), lambda i: (i, 0)) for k in range(2)],
        out_specs=pl.BlockSpec((1, sum(extents)), lambda i: (0, 0)),
        out_shape=jax.ShapeDtypeStruct((1, sum(extents)), F32),
        compiler_params=PARAMS,
    )(*rights, *weights)


def right_product(terms, weights):
    heights, steps = row_blocks(weights)
    extents = [w.shape[0] for w in weights]
    spans = [w.shape[1] for w in weights]
    count = len(terms)

    def kernel(*refs):
        w_refs, (left_ref, out_ref) = refs[count : count + 2], refs[count + 2 :]
        step = pl.program_id(0)

        @pl.when(step == 0)
        def _():
            out_ref[...] = jnp.zeros_like(out_ref)
            left_ref[...] = tree([ref[...] for ref in refs[:count]])

        row = lane = 0
        for k in range(2):
            start = pl.multiple_of(row + step * heights[k], LANES)
            left = left_ref[:, pl.ds(start, heights[k])]
            column = column_of(left.astype(BF16).astype(F32))
            for c in range(0, spans[k], LANES):
                total = jnp.zeros((8, LANES), F32)
                for top in range(0, heights[k], 64):
                    product = w_refs[k][top : top + 64, c : c + LANES].astype(F32) * column[top : top + 64]
                    total += jnp.sum(product.reshape(8, 8, LANES), axis=0)
                out_ref[:, lane + c : lane + c + LANES] += jnp.sum(total, axis=0, keepdims=True)
            squares = left * left
            here = slice(sum(spans) + k * LANES, sum(spans) + (k + 1) * LANES)
            for c in range(0, heights[k], LANES):
                out_ref[:, here] += squares[:, c : c + LANES]
            row += extents[k]
            lane += spans[k]

    total = sum(spans) + 2 * LANES
    return pl.pallas_call(
        kernel,
        grid=(steps,),
        in_specs=[whole(t) for t in terms]
        + [pl.BlockSpec((heights[k], spans[k]), lambda i: (i, 0)) for k in range(2)],
        out_specs=[pl.BlockSpec((1, sum(extents)), lambda i: (0, 0)), pl.BlockSpec((1, total), lambda i: (0, 0))],
        out_shape=[jax.ShapeDtypeStruct((1, sum(extents)), F32), jax.ShapeDtypeStruct((1, total), F32)],
        compiler_params=PARAMS,
    )(*terms, *weights)


def scale_right(total, spans):
    def kernel(total_ref, up_ref, down_ref, squares_ref):
        lane = 0
        for k, ref in enumerate((up_ref, down_ref)):
            here = sum(spans) + k * LANES
            ref[...] = total_ref[:, lane : lane + spans[k]] / norm_of(total_ref[:, here : here + LANES])
            squares = jnp.zeros((1, LANES), F32)
            for c in range(0, spans[k], LANES):
                squares += ref[:, c : c + LANES] * ref[:, c : c + LANES]
            squares_ref[k : k + 1, :] = squares
            lane += spans[k]

    return pl.pallas_call(
        kernel,
        out_shape=[jax.ShapeDtypeStruct((1, span), F32) for span in spans]
        + [jax.ShapeDtypeStruct((2, LANES), F32)],
        compiler_params=PARAMS,
    )(total)


def grad_chunk(order, blocks, inputs, weight, row, columns, buffer, inner, which):
    flat = [array for arrays in blocks for array in arrays]
    count = len(flat)
    tokens = flat[0].shape[0]
    width = sum(array.shape[1] for array in blocks[0])
    depth = inputs.shape[0]
    first, columns = columns
    tile = tile_of(columns, 512)
    chunk, first = row // width, first // tile
    resident = pl.BlockSpec(memory_space=pltpu.VMEM)

    def kernel(order_ref, *refs):
        x_ref, w_ref, before_ref = refs[count : count + 3]
        g_ref, inner_ref, turned = refs[-3:]

        @pl.when(pl.program_id(0) == 0)
        def _():
            inner_ref[...] = before_ref[...]
            position = 0
            for slot, arrays in enumerate(blocks):
                start = pl.multiple_of(order_ref[slot] * tokens, LANES)
                top = 0
                for array in arrays:
                    turned[top : top + array.shape[1], pl.ds(start, tokens)] = refs[position][...].T
                    top += array.shape[1]
                    position += 1

        here = slice(8 * which, 8 * which + 8)
        total = jnp.dot(turned[...], x_ref[...], preferred_element_type=F32)
        start = pl.multiple_of((first + pl.program_id(0)) * tile, LANES)
        g_ref[row : row + width, pl.ds(start, tile)] = total.astype(g_ref.dtype)
        product = total * w_ref[...].astype(F32)
        product = jnp.sum(product.reshape(-1, 8, tile), axis=0)
        inner_ref[here, :] += sum(product[:, c : c + LANES] for c in range(0, tile, LANES))

    in_specs = [pl.BlockSpec(array.shape, lambda j, o: (0, 0)) for array in flat]
    in_specs += [
        pl.BlockSpec((depth, tile), lambda j, o: (0, first + j)),
        pl.BlockSpec((width, tile), lambda j, o: (chunk, first + j)),
        whole(inner),
    ]
    operands = [order, *flat, inputs, weight, inner]
    aliases = {}
    if buffer is not None:
        in_specs.append(resident)
        operands.append(buffer)
        aliases = {count + 4: 0}
    return pl.pallas_call(
        kernel,
        grid_spec=pltpu.PrefetchScalarGridSpec(
            num_scalar_prefetch=1,
            grid=(columns // tile,),
            in_specs=in_specs,
            out_specs=[
                resident,
                whole(inner),
            ],
            scratch_shapes=[pltpu.VMEM((width, depth), BF16)],
        ),
        out_shape=[
            pltpu.VMEM(weight.shape, BF16),
            jax.ShapeDtypeStruct(inner.shape, F32),
        ],
        input_output_aliases=aliases,
        compiler_params=pltpu.CompilerParams(vmem_limit_bytes=36 * 1024 * 1024),
        cost_estimate=pl.CostEstimate(
            flops=2 * depth * width * columns,
            bytes_accessed=2 * (depth * width + depth * columns + 2 * width * columns),
            transcendentals=0,
        ),
    )(*operands)


def finish(grads, left, norms, rights, terms, factors):
    heights, steps = row_blocks(grads)
    extents = [g.shape[0] for g in grads]
    spans = [g.shape[1] for g in grads]
    count = len(terms)

    def kernel(factors_ref, left_ref, norms_ref, *refs):
        right_refs, refs = refs[:2], refs[2:]
        term_refs, refs = refs[:count], refs[count:]
        g_refs, out_refs, gain_ref, v_refs = refs[:2], refs[2:4], refs[4], refs[5:]
        step = pl.program_id(0)

        @pl.when(step == 0)
        def _():
            total = tree([ref[...] for ref in term_refs])
            for k in range(2):
                gain, sigma = factors_ref[0, k], factors_ref[1, k]
                gw = jnp.sum(total[8 * k : 8 * k + 8])
                gain_ref[k] = gw / sigma
                v_refs[k][...] = gain * gw / (sigma * sigma) * right_refs[k][...]

        row = 0
        for k in range(2):
            scale = factors_ref[0, k] / factors_ref[1, k]
            top = pl.multiple_of(step * heights[k], LANES)
            start = pl.multiple_of(row + step * heights[k], LANES)
            norm = norm_of(norms_ref[:, k * LANES : (k + 1) * LANES])
            column = column_of((left_ref[:, pl.ds(start, heights[k])] / norm).astype(BF16).astype(F32))
            for r in range(0, heights[k], 64):
                part = column[r : r + 64]
                for c in range(0, spans[k], LANES):
                    here = slice(c, c + LANES)
                    g = g_refs[k][pl.ds(top + r, 64), here].astype(F32)
                    out_refs[k][r : r + 64, here] = (scale * g - part * v_refs[k][:, here]).astype(BF16)
            row += extents[k]

    operands = [left, norms, *rights, *terms]
    blocks = [pl.BlockSpec((heights[k], spans[k]), lambda i: (i, 0)) for k in range(2)]
    smem = pl.BlockSpec(memory_space=pltpu.SMEM)
    return pl.pallas_call(
        kernel,
        grid=(steps,),
        in_specs=[smem] + [whole(o) for o in operands] + [pl.BlockSpec(memory_space=pltpu.VMEM)] * 2,
        out_specs=blocks + [smem],
        out_shape=[jax.ShapeDtypeStruct(g.shape, BF16) for g in grads] + [jax.ShapeDtypeStruct((2,), F32)],
        scratch_shapes=[pltpu.VMEM((1, span), F32) for span in spans],
        compiler_params=pltpu.CompilerParams(vmem_limit_bytes=36 * 1024 * 1024),
    )(factors, *operands, *grads)


def local(
    rows,
    cols,
    gain_pair,
    weight_up,
    weight_down,
    inputs_up,
    grads_up,
    inputs_down,
    grads_down,
    vector_up,
    vector_down,
):
    weights = (weight_up, weight_down)
    inputs = [lax.all_gather(array, "row", axis=0, tiled=True) for array in (inputs_up, inputs_down)]
    extents = (weight_up.shape[0], weight_down.shape[0])
    spans = (weight_up.shape[1], weight_down.shape[1])
    ring = [(i, (i + 1) % cols) for i in range(cols)]
    order = lax.rem(lax.axis_index("col") - jnp.arange(cols, dtype=jnp.int32) + cols, jnp.int32(cols))

    third = grads_up.shape[1] // 3
    held = {name: [grads_up[:, c * third : (c + 1) * third]] for c, name in enumerate("uvc")}
    held["d"] = [grads_down]

    def send(*names):
        for name in names:
            held[name].append(lax.ppermute(held[name][-1], "col", ring))

    def when(names, *values):
        got, *values = fence([held[name][-1] for name in names], *values)
        for name, block in zip(names, got):
            held[name][-1] = block
        return values if len(values) > 1 else values[0]

    grads = [None, None]

    def multiply(k, names, row, inner, part=0, parts=1):
        blocks = list(zip(*(held[name] for name in names)))
        columns = (part * spans[k] // parts, spans[k] // parts)
        grads[k], inner = grad_chunk(order, blocks, inputs[k], weights[k], row, columns, grads[k], inner, k)
        return inner

    send("d", "u")
    part = left_product((vector_up[None, :], vector_down[None, :]), weights)
    terms = exchange(part, "col", cols)
    terms = when("du", terms)
    send("d", "u")
    left, total = right_product(terms, weights)
    total = when("d", all_sum(total, "row", rows))
    send("d")
    *rights, _ = scale_right(total, spans)
    part = left_product(rights, weights)
    terms = exchange(part, "col", cols)
    terms = when("udvc", terms)
    send("u", "v", "c")
    left, total = right_product(terms, weights)
    total = when("u", all_sum(total, "row", rows))
    *rights, square = scale_right(total, spans)
    squares = exchange(square, "col", cols)
    inner = jnp.zeros((16, LANES), F32)
    for _ in range(cols - 4):
        inner = when("udvc", inner)
        send("u", "d", "v", "c")
    inner = when("v", inner)
    send("v")
    inner = multiply(0, "u", 0, inner)
    inner, squares = when("c", inner, squares)
    send("c")
    norms = total[:, sum(spans) :]
    norm = jnp.sqrt(jnp.sum(norms.reshape(2, LANES), axis=1) + EPS)
    sigma = jnp.sqrt(jnp.sum(tree(squares), axis=1) + EPS)
    vectors = [left[0, : extents[0]] / norm[0], left[0, extents[0] :] / norm[1]]
    rights = [rights[k] / sigma[k] for k in range(2)]
    vectors += [row[0] for row in rights]
    inner = multiply(1, "d", 0, inner, 0, 2)
    inner, vectors, rights, sigma = when("v", inner, vectors, rights, sigma)
    send("v")
    inner = multiply(1, "d", 0, inner, 1, 2)
    inner = when("c", inner)
    send("c")
    inner = when("v", inner)
    inner = multiply(0, "v", third, inner)
    inner = when("c", inner)
    inner = multiply(0, "c", 2 * third, inner)
    terms = exchange(all_sum(inner, "row", rows), "col", cols)
    factors = jnp.stack([gain_pair, sigma])
    wgrad_up, wgrad_down, gain_grads = finish(grads, left, norms, rights, terms, factors)
    left_up, left_down, right_up, right_down = vectors
    return wgrad_up, wgrad_down, gain_grads, left_up, right_up, left_down, right_down


def solution(mesh):
    in_specs = (
        P(),
        P("row", "col"),
        P("row", "col"),
        P("row", "col"),
        P("col", "row"),
        P("row", "col"),
        P("col", "row"),
        P("col"),
        P("col"),
    )
    out_specs = (P("row", "col"), P("row", "col"), P(), P("row"), P("col"), P("row"), P("col"))
    body = functools.partial(local, mesh.shape["row"], mesh.shape["col"])
    return jax.shard_map(body, mesh=mesh, in_specs=in_specs, out_specs=out_specs, check_vma=False)
```

```python
import functools

import jax
import jax.numpy as jnp
from jax import lax
from jax.experimental import pallas as pl
from jax.experimental.pallas import tpu as pltpu
from jax.sharding import PartitionSpec as P

EPS = 1e-06
LANES = 128
PARAMS = pltpu.CompilerParams(vmem_limit_bytes=28 * 1024 * 1024)
F32 = jnp.float32
BF16 = jnp.bfloat16


def exchange(value, axis, size, stride=1):
    return [value] + [
        lax.ppermute(value, axis, [(i, i ^ k) for i in range(size)]) for k in range(stride, size, stride)
    ]


def tree(terms):
    while len(terms) > 1:
        terms = [terms[i] + terms[i + 1] for i in range(0, len(terms), 2)]
    return terms[0]


def all_sum(value, axis, size):
    step = 1
    while step < size:
        value = value + lax.ppermute(value, axis, [(i, i ^ step) for i in range(size)])
        step *= 2
    return value


def quick_sum(value, axis, size):
    pair = value + lax.ppermute(value, axis, [(i, i ^ 1) for i in range(size)])
    return tree(exchange(pair, axis, size, 2))


def fence(*values):
    return lax.optimization_barrier(values)


def tile_of(extent, most):
    tile = min(extent, most)
    while extent % tile:
        tile -= LANES
    return tile


def column_of(row):
    return jnp.broadcast_to(row, (LANES, row.shape[1])).T


def row_of(block):
    return jnp.sum(block.T, axis=0, keepdims=True)


def norm_of(squares):
    return jnp.sqrt(jnp.sum(squares, axis=1, keepdims=True) + EPS)


def whole(array):
    return pl.BlockSpec(array.shape, lambda *_: (0,) * array.ndim)


def row_blocks(weights):
    steps = weights[1].shape[0] // LANES
    return [w.shape[0] // steps for w in weights], steps


def left_product(rights, weights):
    heights, steps = row_blocks(weights)
    extents = [w.shape[0] for w in weights]

    def kernel(v_up_ref, v_down_ref, w_up_ref, w_down_ref, out_ref):
        step = pl.program_id(0)
        offset = 0
        for k, (w_ref, v_ref) in enumerate(((w_up_ref, v_up_ref), (w_down_ref, v_down_ref))):
            height, depth = w_ref.shape
            sums = []
            for top in range(0, height, 64):
                total = jnp.zeros((64, LANES), F32)
                for c in range(0, depth, LANES):
                    v = v_ref[:, c : c + LANES].astype(BF16).astype(F32)
                    total += w_ref[top : top + 64, c : c + LANES].astype(F32) * v
                sums.append(total)
            start = pl.multiple_of(offset + step * height, LANES)
            out_ref[:, pl.ds(start, height)] = row_of(jnp.concatenate(sums))
            offset += extents[k]

    return pl.pallas_call(
        kernel,
        grid=(steps,),
        in_specs=[whole(r) for r in rights]
        + [pl.BlockSpec((heights[k], weights[k].shape[1]), lambda i: (i, 0)) for k in range(2)],
        out_specs=pl.BlockSpec((1, sum(extents)), lambda i: (0, 0)),
        out_shape=jax.ShapeDtypeStruct((1, sum(extents)), F32),
        compiler_params=PARAMS,
    )(*rights, *weights)


def right_product(terms, weights):
    heights, steps = row_blocks(weights)
    extents = [w.shape[0] for w in weights]
    spans = [w.shape[1] for w in weights]
    count = len(terms)

    def kernel(*refs):
        w_refs, (left_ref, out_ref) = refs[count : count + 2], refs[count + 2 :]
        step = pl.program_id(0)

        @pl.when(step == 0)
        def _():
            out_ref[...] = jnp.zeros_like(out_ref)
            left_ref[...] = tree([ref[...] for ref in refs[:count]])

        row = lane = 0
        for k in range(2):
            start = pl.multiple_of(row + step * heights[k], LANES)
            left = left_ref[:, pl.ds(start, heights[k])]
            column = column_of(left.astype(BF16).astype(F32))
            for c in range(0, spans[k], LANES):
                total = jnp.zeros((8, LANES), F32)
                for top in range(0, heights[k], 64):
                    product = w_refs[k][top : top + 64, c : c + LANES].astype(F32) * column[top : top + 64]
                    total += jnp.sum(product.reshape(8, 8, LANES), axis=0)
                out_ref[:, lane + c : lane + c + LANES] += jnp.sum(total, axis=0, keepdims=True)
            squares = left * left
            here = slice(sum(spans) + k * LANES, sum(spans) + (k + 1) * LANES)
            for c in range(0, heights[k], LANES):
                out_ref[:, here] += squares[:, c : c + LANES]
            row += extents[k]
            lane += spans[k]

    total = sum(spans) + 2 * LANES
    return pl.pallas_call(
        kernel,
        grid=(steps,),
        in_specs=[whole(t) for t in terms]
        + [pl.BlockSpec((heights[k], spans[k]), lambda i: (i, 0)) for k in range(2)],
        out_specs=[pl.BlockSpec((1, sum(extents)), lambda i: (0, 0)), pl.BlockSpec((1, total), lambda i: (0, 0))],
        out_shape=[jax.ShapeDtypeStruct((1, sum(extents)), F32), jax.ShapeDtypeStruct((1, total), F32)],
        compiler_params=PARAMS,
    )(*terms, *weights)


def scale_right(total, spans):
    def kernel(total_ref, up_ref, down_ref, squares_ref):
        lane = 0
        for k, ref in enumerate((up_ref, down_ref)):
            here = sum(spans) + k * LANES
            ref[...] = total_ref[:, lane : lane + spans[k]] / norm_of(total_ref[:, here : here + LANES])
            squares = jnp.zeros((1, LANES), F32)
            for c in range(0, spans[k], LANES):
                squares += ref[:, c : c + LANES] * ref[:, c : c + LANES]
            squares_ref[k : k + 1, :] = squares
            lane += spans[k]

    return pl.pallas_call(
        kernel,
        out_shape=[jax.ShapeDtypeStruct((1, span), F32) for span in spans]
        + [jax.ShapeDtypeStruct((2, LANES), F32)],
        compiler_params=PARAMS,
    )(total)


def grad_chunk(order, blocks, inputs, weight, row, columns, buffer, inner, which):
    flat = [array for arrays in blocks for array in arrays]
    count = len(flat)
    tokens = flat[0].shape[0]
    width = sum(array.shape[1] for array in blocks[0])
    depth = inputs.shape[0]
    first, columns = columns
    tile = tile_of(columns, 512)
    chunk, first = row // width, first // tile
    resident = pl.BlockSpec(memory_space=pltpu.VMEM)

    def kernel(order_ref, *refs):
        x_ref, w_ref, before_ref = refs[count : count + 3]
        g_ref, inner_ref, turned = refs[-3:]

        @pl.when(pl.program_id(0) == 0)
        def _():
            inner_ref[...] = before_ref[...]
            position = 0
            for slot, arrays in enumerate(blocks):
                start = pl.multiple_of(order_ref[slot] * tokens, LANES)
                top = 0
                for array in arrays:
                    turned[top : top + array.shape[1], pl.ds(start, tokens)] = refs[position][...].T
                    top += array.shape[1]
                    position += 1

        total = jnp.dot(turned[...], x_ref[...], preferred_element_type=F32)
        start = pl.multiple_of((first + pl.program_id(0)) * tile, LANES)
        g_ref[row : row + width, pl.ds(start, tile)] = total.astype(g_ref.dtype)
        product = total * w_ref[...].astype(F32)
        product = jnp.sum(product.reshape(-1, 8, tile), axis=0)
        inner_ref[8 * which : 8 * which + 8, :] += sum(product[:, c : c + LANES] for c in range(0, tile, LANES))

    in_specs = [pl.BlockSpec(array.shape, lambda j, o: (0, 0)) for array in flat]
    in_specs += [
        pl.BlockSpec((depth, tile), lambda j, o: (0, first + j)),
        pl.BlockSpec((width, tile), lambda j, o: (chunk, first + j)),
        whole(inner),
    ]
    large = [pltpu.with_memory_space_constraint(array, pltpu.HBM) for array in (*flat, inputs, weight)]
    operands = [order, *large, inner]
    aliases = {}
    if buffer is not None:
        in_specs.append(resident)
        operands.append(buffer)
        aliases = {count + 4: 0}
    return pl.pallas_call(
        kernel,
        grid_spec=pltpu.PrefetchScalarGridSpec(
            num_scalar_prefetch=1,
            grid=(columns // tile,),
            in_specs=in_specs,
            out_specs=[
                resident,
                whole(inner),
            ],
            scratch_shapes=[pltpu.VMEM((width, depth), BF16)],
        ),
        out_shape=[
            pltpu.VMEM(weight.shape, BF16),
            jax.ShapeDtypeStruct(inner.shape, F32),
        ],
        input_output_aliases=aliases,
        compiler_params=pltpu.CompilerParams(vmem_limit_bytes=36 * 1024 * 1024),
        cost_estimate=pl.CostEstimate(
            flops=2 * depth * width * columns,
            bytes_accessed=2 * (depth * width + depth * columns + 2 * width * columns),
            transcendentals=0,
        ),
    )(*operands)


def finish(grads, lefts, rights, terms, factors):
    heights, steps = row_blocks(grads)
    spans = [g.shape[1] for g in grads]
    count = len(terms)

    def kernel(factors_ref, *refs):
        right_refs, term_refs, refs = refs[:2], refs[2 : count + 2], refs[count + 2 :]
        left_refs, g_refs, out_refs, gain_ref, v_refs = refs[:2], refs[2:4], refs[4:6], refs[6], refs[7:]

        @pl.when(pl.program_id(0) == 0)
        def _():
            total = tree([ref[...] for ref in term_refs])
            for k in range(2):
                gain, sigma = factors_ref[0, k], factors_ref[1, k]
                gw = jnp.sum(total[8 * k : 8 * k + 8])
                gain_ref[k] = gw / sigma
                v_refs[k][...] = gain * gw / (sigma * sigma) * right_refs[k][...]

        for k in range(2):
            scale = factors_ref[0, k] / factors_ref[1, k]
            for r in range(0, heights[k], 64):
                part = left_refs[k][r : r + 64]
                for c in range(0, spans[k], LANES):
                    here = slice(c, c + LANES)
                    g = g_refs[k][r : r + 64, here].astype(F32)
                    out_refs[k][r : r + 64, here] = (scale * g - part * v_refs[k][:, here]).astype(BF16)

    operands = [*rights, *terms]
    blocks = [pl.BlockSpec((heights[k], spans[k]), lambda i: (i, 0)) for k in range(2)]
    smem = pl.BlockSpec(memory_space=pltpu.SMEM)
    return pl.pallas_call(
        kernel,
        grid=(steps,),
        in_specs=[smem]
        + [whole(o) for o in operands]
        + [pl.BlockSpec((heights[k], LANES), lambda i: (i, 0)) for k in range(2)]
        + blocks,
        out_specs=blocks + [smem],
        out_shape=[jax.ShapeDtypeStruct(g.shape, BF16) for g in grads] + [jax.ShapeDtypeStruct((2,), F32)],
        scratch_shapes=[pltpu.VMEM((1, span), F32) for span in spans],
        compiler_params=pltpu.CompilerParams(vmem_limit_bytes=24 * 1024 * 1024),
    )(factors, *operands, *lefts, *[pltpu.with_memory_space_constraint(g, pltpu.VMEM) for g in grads])


def local(
    rows,
    cols,
    gain_pair,
    weight_up,
    weight_down,
    inputs_up,
    grads_up,
    inputs_down,
    grads_down,
    vector_up,
    vector_down,
):
    weights = (weight_up, weight_down)
    all_down = lax.all_gather(inputs_down, "row", axis=0, tiled=True)
    inputs = [lax.all_gather(inputs_up, "row", axis=0, tiled=True), all_down]
    extents = (weight_up.shape[0], weight_down.shape[0])
    spans = (weight_up.shape[1], weight_down.shape[1])
    ring = [(i, (i + 1) % cols) for i in range(cols)]
    order = lax.rem(lax.axis_index("col") - jnp.arange(cols, dtype=jnp.int32) + cols, jnp.int32(cols))

    third = grads_up.shape[1] // 3
    held = {"u": [grads_up[:, :third]]}
    held["d"] = [grads_down]

    def send(*names):
        for name in names:
            held[name].append(lax.ppermute(held[name][-1], "col", ring))

    def when(names, *values):
        got, *values = fence([held[name][-1] for name in names], *values)
        for name, block in zip(names, got):
            held[name][-1] = block
        return values if len(values) > 1 else values[0]

    grads = [None, None]

    def multiply(k, names, row, inner, part=0, parts=1):
        blocks = list(zip(*(held[name] for name in names)))
        columns = (part * spans[k] // parts, spans[k] // parts)
        grads[k], inner = grad_chunk(order, blocks, inputs[k], weights[k], row, columns, grads[k], inner, k)
        return inner

    send("d", "u")
    part = left_product((vector_up[None, :], vector_down[None, :]), weights)
    terms = exchange(part, "col", cols)
    later, _ = fence(grads_up, part)
    held["v"], held["c"] = [later[:, third : 2 * third]], [later[:, 2 * third :]]
    terms = when("du", terms)
    send("d", "u")
    left, total = right_product(terms, weights)
    total = when("d", all_sum(total, "row", rows))
    send("d")
    *rights, _ = scale_right(total, spans)
    part = left_product(rights, weights)
    terms = exchange(part, "col", cols)
    terms = when("udvc", terms)
    send("u", "v", "c")
    left, total = right_product(terms, weights)
    total = when("u", all_sum(total, "row", rows))
    *rights, square = scale_right(total, spans)
    squares = exchange(square, "col", cols)
    inner = jnp.zeros((16, LANES), F32)
    for _ in range(cols - 4):
        inner = when("udvc", inner)
        send("u", "d", "v", "c")
    inner = when("v", inner)
    send("v")
    inner = multiply(1, "d", 0, inner, 0, 2)
    inner, squares = when("c", inner, squares)
    send("c")
    norms = total[:, sum(spans) :]
    norm = jnp.sqrt(jnp.sum(norms.reshape(2, LANES), axis=1) + EPS)
    lefts = [left[0, : extents[0]] / norm[0], left[0, extents[0] :] / norm[1]]
    columns = [jnp.broadcast_to(u.astype(BF16).astype(F32)[:, None], (u.shape[0], LANES)) for u in lefts]
    sigma = jnp.sqrt(jnp.sum(tree(squares), axis=1) + EPS)
    rights = [rights[k] / sigma[k] for k in range(2)]
    vectors = lefts + [row[0] for row in rights]
    factors = jnp.stack([gain_pair, sigma])
    inner = multiply(1, "d", 0, inner, 1, 2)
    inner, vectors, rights, factors, columns = when("v", inner, vectors, rights, factors, columns)
    send("v")
    inner = multiply(0, "u", 0, inner)
    inner = when("c", inner)
    send("c")
    inner = when("v", inner)
    inner = multiply(0, "v", third, inner)
    inner = when("c", inner)
    inner = multiply(0, "c", 2 * third, inner)
    terms = exchange(quick_sum(inner, "row", rows), "col", cols)
    wgrad_up, wgrad_down, gain_grads = finish(grads, columns, rights, terms, factors)
    left_up, left_down, right_up, right_down = vectors
    return wgrad_up, wgrad_down, gain_grads, left_up, right_up, left_down, right_down


def solution(mesh):
    in_specs = (
        P(),
        P("row", "col"),
        P("row", "col"),
        P("row", "col"),
        P("col", "row"),
        P("row", "col"),
        P("col", "row"),
        P("col"),
        P("col"),
    )
    out_specs = (P("row", "col"), P("row", "col"), P(), P("row"), P("col"), P("row"), P("col"))
    body = functools.partial(local, mesh.shape["row"], mesh.shape["col"])
    return jax.shard_map(body, mesh=mesh, in_specs=in_specs, out_specs=out_specs, check_vma=False)
```
